256 devices in a mesh: section: 4 (over y), dp: 16 (over z_hi, x, core), tensor: 4 (over z_lo).
Axes of the slice: x: 4, y: 4, z: 8 (z_hi: 2, z_lo: 4; z = z_hi * 4 + z_lo), core: 2. Of those that a mesh axis runs over, the one named last changes fastest.
Arguments:
- query_grads: bfloat16 [4, 16, 128, 15872], P('section', 'dp', None, 'tensor'), may hold values from -450 to 450
- query_master: float32 [4, 128, 15872], P('section', 'dp', 'tensor'), may hold values from -5 to 5
- query_first: float32 [4, 128, 15872], P('section', 'dp', 'tensor'), may hold values from -3 to 3
- query_second: float32 [4, 128, 15872], P('section', 'dp', 'tensor'), may hold values from 0.01 to 1
- output_grads: bfloat16 [4, 16, 256, 14848], P('section', 'dp', 'tensor'), may hold values from -450 to 450
- output_master: float32 [4, 256, 14848], P('section', 'tensor', 'dp'), may hold values from -5 to 5
- output_first: float32 [4, 256, 14848], P('section', 'tensor', 'dp'), may hold values from -3 to 3
- output_second: float32 [4, 256, 14848], P('section', 'tensor', 'dp'), may hold values from 0.01 to 1
- table_grads: bfloat16 [4, 16, 256, 14848], P('section', 'dp', 'tensor'), may hold values from -450 to 450
- table_master: float32 [256, 14848], P('tensor', ('section', 'dp')), may hold values from -5 to 5
- table_first: float32 [256, 14848], P('tensor', ('section', 'dp')), may hold values from -3 to 3
- table_second: float32 [256, 14848], P('tensor', ('section', 'dp')), may hold values from 0.01 to 1
Outputs:
- query_weights: bfloat16 [4, 128, 15872], P('section', None, 'tensor')
- query_updated: float32 [4, 128, 15872], P('section', 'dp', 'tensor')
- query_moment: float32 [4, 128, 15872], P('section', 'dp', 'tensor')
- query_variance: float32 [4, 128, 15872], P('section', 'dp', 'tensor')
- output_weights: bfloat16 [4, 256, 14848], P('section', 'tensor')
- output_updated: float32 [4, 256, 14848], P('section', 'tensor', 'dp')
- output_moment: float32 [4, 256, 14848], P('section', 'tensor', 'dp')
- output_variance: float32 [4, 256, 14848], P('section', 'tensor', 'dp')
- table_weights: bfloat16 [256, 14848], P('tensor')
- table_updated: float32 [256, 14848], P('tensor', ('section', 'dp'))
- table_moment: float32 [256, 14848], P('tensor', ('section', 'dp'))
- table_variance: float32 [256, 14848], P('tensor', ('section', 'dp'))
The draws below stay inside these ranges and needn't reach their ends.
All inputs are finite; a program needn't handle non-finite values.
Results may differ from the reference program's by a relative error of at most 0.001.
Values may be sent and summed in bfloat16 or wider, within the bound.
No kernel may reach another device: no remote copies, remote signals or barrier semaphores. Data moves between devices by JAX's collectives and lax.ppermute only.
A program may use at most 128 MiB of HBM per device.

```python
import math
import jax
import jax.numpy as jnp

D = 14848
QROWS = 128
STEP = 10
QKVCOLS = 15872
OROWS = 256
EROWS = 256
PARAMS = 27131904
N_SECTION = 4
N_DP = 16


def scale_partials(key, noise, ramp_dim):
    shape = noise.shape
    key_rows, key_cols = jax.random.split(key, 2)
    row_scale = jnp.exp(math.log(10.0) * jax.random.uniform(key_rows, (1, 1, shape[2], 1), jnp.float32))
    col_scale = jnp.exp(math.log(10.0) * jax.random.uniform(key_cols, (1, 1, 1, shape[3]), jnp.float32))
    section_pos = jnp.arange(shape[0], dtype=jnp.float32) / max(shape[0] - 1, 1)
    section_ramp = jnp.exp(math.log(3.0) * section_pos).reshape(shape[0], 1, 1, 1)
    count = shape[ramp_dim]
    owner_pos = jnp.arange(count, dtype=jnp.float32) / max(count - 1, 1)
    ramp_shape = [1, 1, 1, 1]
    ramp_shape[ramp_dim] = count
    owner_ramp = jnp.exp(math.log(3.0) * owner_pos).reshape(ramp_shape)
    return 0.1 * noise * row_scale * col_scale * section_ramp * owner_ramp


def draw_query_grads(key, part):
    key = jax.random.fold_in(key, 11)
    key_noise = jax.random.fold_in(key, 0)
    key_scale = jax.random.fold_in(key, 2)
    shape = (N_SECTION, N_DP, QROWS, QKVCOLS)
    noise = jnp.clip(jax.random.normal(key_noise, shape, jnp.float32), -5.0, 5.0)
    return scale_partials(key_scale, noise, 2).astype(jnp.bfloat16)


def draw_output_grads(key, part):
    key = jax.random.fold_in(key, 23)
    key_noise = jax.random.fold_in(key, 0)
    key_scale = jax.random.fold_in(key, 2)
    shape = (N_SECTION, N_DP, OROWS, D)
    noise = jnp.clip(jax.random.normal(key_noise, shape, jnp.float32), -5.0, 5.0)
    return scale_partials(key_scale, noise, 3).astype(jnp.bfloat16)


def draw_table_grads(key, part):
    key = jax.random.fold_in(key, 37)
    key_noise = jax.random.fold_in(key, 0)
    key_scale = jax.random.fold_in(key, 2)
    shape = (N_SECTION, N_DP, EROWS, D)
    noise = jnp.clip(jax.random.normal(key_noise, shape, jnp.float32), -5.0, 5.0)
    return scale_partials(key_scale, noise, 3).astype(jnp.bfloat16)


def shard_levels(stream_key, shape, shards, least, top_value):
    loudness, own = 1.0, jax.random.fold_in(stream_key, 6)
    for position, blocks in shards:
        heights = jnp.exp(jax.random.uniform(jax.random.fold_in(own, position), (blocks,), jnp.float32, least / len(shards), top_value / len(shards)))
        loudness = loudness * jnp.repeat(heights, shape[position] // blocks).reshape([-1 if axis == position else 1 for axis in range(len(shape))])
    return loudness


def centred(rng, shape, spread, most, shards=(), kind=jnp.bfloat16):
    drawn = jax.random.normal(rng, shape, jnp.float32) * spread
    if len(shards) > 0:
        drawn = shard_levels(rng, shape, shards, -0.22, 0.18) * drawn
    return jnp.clip(drawn, min=-most, max=most).astype(kind)


def setup_inputs(seed: int = 0) -> dict:
    seeds = jax.random.split(jax.random.key(seed), 13)
    query_grads = draw_query_grads(jax.random.fold_in(seeds[12], 71), 0)
    query_master = centred(seeds[1], (N_SECTION, QROWS, QKVCOLS), 1.0, 5.0, ((0, 4), (1, 16), (2, 4)), jnp.float32)
    query_first = centred(seeds[2], (N_SECTION, QROWS, QKVCOLS), 0.5, 3.0, ((0, 4), (1, 16), (2, 4)), jnp.float32)
    query_second = jnp.clip(jnp.exp(math.log(1.0) - 4.6051702 * jax.random.uniform(seeds[3], (N_SECTION, QROWS, QKVCOLS), jnp.float32) ** shard_levels(seeds[3], (N_SECTION, QROWS, QKVCOLS), ((0, 4), (1, 16), (2, 4)), -0.2, 0.2)), 0.01, 1.0)
    output_grads = draw_output_grads(jax.random.fold_in(seeds[12], 71), 0)
    output_master = centred(seeds[5], (N_SECTION, OROWS, D), 1.0, 5.0, ((0, 4), (1, 4), (2, 16)), jnp.float32)
    output_first = centred(seeds[6], (N_SECTION, OROWS, D), 0.5, 3.0, ((0, 4), (1, 4), (2, 16)), jnp.float32)
    output_second = jnp.clip(jnp.exp(math.log(1.0) - 4.6051702 * jax.random.uniform(seeds[7], (N_SECTION, OROWS, D), jnp.float32) ** shard_levels(seeds[7], (N_SECTION, OROWS, D), ((0, 4), (1, 4), (2, 16)), -0.2, 0.2)), 0.01, 1.0)
    table_grads = draw_table_grads(jax.random.fold_in(seeds[12], 71), 0)
    table_master = centred(seeds[9], (EROWS, D), 1.0, 5.0, ((0, 4), (1, 64)), jnp.float32)
    table_first = centred(seeds[10], (EROWS, D), 0.5, 3.0, ((0, 4), (1, 64)), jnp.float32)
    table_second = jnp.clip(jnp.exp(math.log(1.0) - 4.6051702 * jax.random.uniform(seeds[11], (EROWS, D), jnp.float32) ** shard_levels(seeds[11], (EROWS, D), ((0, 4), (1, 64)), -0.2, 0.2)), 0.01, 1.0)
    return dict(query_grads=query_grads, query_master=query_master, query_first=query_first, query_second=query_second, output_grads=output_grads, output_master=output_master, output_first=output_first, output_second=output_second, table_grads=table_grads, table_master=table_master, table_first=table_first, table_second=table_second)


beta_first = 0.9
beta_second = 0.95
learn_rate = 0.02
weight_decay = 0.1
tiny_value = 1e-08

def member_sum(partials):
    total = partials[:, 0].astype(jnp.float32)
    for member in range(1, partials.shape[1]):
        total = total + partials[:, member].astype(jnp.float32)
    return total

def adamw(gradient, master, first, second, factor):
    clipped = gradient * factor
    first_new = beta_first * first + (1.0 - beta_first) * clipped
    second_new = beta_second * second + (1.0 - beta_second) * clipped * clipped
    first_hat = first_new / (1.0 - beta_first ** STEP)
    second_hat = second_new / (1.0 - beta_second ** STEP)
    master_new = master - learn_rate * (first_hat / (jnp.sqrt(second_hat) + tiny_value) + weight_decay * master)
    return (master_new, first_new, second_new)

def reference(query_grads, query_master, query_first, query_second, output_grads, output_master, output_first, output_second, table_grads, table_master, table_first, table_second):
    query_sum = member_sum(query_grads)
    output_sum = member_sum(output_grads)
    table_sum = table_grads[0, 0].astype(jnp.float32) + table_grads[N_SECTION - 1, 0].astype(jnp.float32)
    for member in range(1, N_DP):
        table_sum = table_sum + (table_grads[0, member].astype(jnp.float32) + table_grads[N_SECTION - 1, member].astype(jnp.float32))
    squares = jnp.sum(query_sum * query_sum) + jnp.sum(output_sum * output_sum) + jnp.sum(table_sum * table_sum)
    grad_norm = jnp.sqrt(squares)
    factor = jnp.minimum(jnp.float32(1.0), 0.5 * math.sqrt(PARAMS) / (grad_norm + 1e-06))
    query_new, query_mom, query_var = adamw(query_sum, query_master, query_first, query_second, factor)
    output_new, output_mom, output_var = adamw(output_sum, output_master, output_first, output_second, factor)
    table_new, table_mom, table_var = adamw(table_sum, table_master, table_first, table_second, factor)
    return (query_new.astype(jnp.bfloat16), query_new, query_mom, query_var, output_new.astype(jnp.bfloat16), output_new, output_mom, output_var, table_new.astype(jnp.bfloat16), table_new, table_mom, table_var)
```

```python
import math

import jax
import jax.numpy as jnp
from jax import lax
from jax.experimental import pallas as pl
from jax.experimental.pallas import tpu as pltpu
from jax.sharding import PartitionSpec as P

STEP = 10

beta_first = 0.9
beta_second = 0.95
learn_rate = 0.02
weight_decay = 0.1
tiny_value = 1e-08

F32, BF16, F16 = jnp.float32, jnp.bfloat16, jnp.float16

QT = 31
QROWS, OROWS, TROWS = 248, 464, 128
SUMS = QROWS + OROWS
WQ = 256
WEIGHTS = WQ + OROWS
PARAMS_KERNEL = pltpu.CompilerParams(vmem_limit_bytes=40 * 1024 * 1024)


def pair_perm(move):
    return [(d, move(d)) for d in range(16)]


CORE = pair_perm(lambda d: d ^ 1)
ZHALF = pair_perm(lambda d: d ^ 8)


def x_perm(k):
    return pair_perm(lambda d: (d & 9) | ((((d >> 1) + k) & 3) << 1))


def ring_perm(k):
    return [(i, (i + k) % 4) for i in range(4)]


def lanes(rows):
    return lax.broadcasted_iota(jnp.int32, (rows, 128), 1)


def call(kernel, outs, *args):
    return pl.pallas_call(kernel, out_shape=outs, compiler_params=PARAMS_KERNEL)(*args)


def out(shape, dtype):
    return jax.ShapeDtypeStruct(shape, dtype)


def position():
    d = lax.axis_index("dp")
    return d // 8, (d // 2) % 4, d % 2


def split_kernel(q_ref, o_ref, qs_ref, os_ref):
    _, _, core = position()
    other = 1 - core

    def rows(j, carry):
        r = pl.multiple_of(j * 32, 32)
        v = q_ref[pl.ds(r, 32), :].astype(F32)
        first = jnp.where(other == 0, v[0:8], v[8:16])
        second = jnp.where(other == 0, v[16:24], v[24:32])
        qs_ref[pl.ds(pl.multiple_of(j * 16, 16), 16), :] = jnp.concatenate(
            [first, second], axis=0
        ).astype(BF16)
        return carry

    lax.fori_loop(0, 4, rows, 0)

    def cols(j, carry):
        start = pl.multiple_of(((29 * (2 * j + other)) // 4) * 128, 128)
        os_ref[j] = o_ref[:, pl.ds(start, 1024)]
        return carry

    lax.fori_loop(0, 8, cols, 0)


def pack_kernel(q_ref, o_ref, qr_ref, or_ref, out_ref):
    _, x, core = position()
    lane = lanes(64)
    lane16 = lanes(16)

    def block(j, carry):
        half, xb = j // 4, j % 4
        slot = (xb - x + 4) % 4
        v = q_ref[pl.ds(pl.multiple_of(j * 16, 16), 16), :].astype(F32)
        w = qr_ref[pl.ds(pl.multiple_of((j // 2) * 16, 16), 16), :].astype(F32)
        total = jnp.where(core == 0, v[0:8], v[8:16]) + jnp.where(j % 2 == 0, w[0:8], w[8:16])
        for t in range(QT):
            out_ref[slot, half, 8 * t : 8 * t + 8, :] = total[:, 128 * t : 128 * t + 128]
        d = 2 * j + core
        start = pl.multiple_of(((29 * d) // 4) * 128, 128)
        shift = 32 * (d % 4)
        turn = (128 - shift) % 128
        tiles = []
        for t in range(8):
            a = o_ref[:, pl.ds(start + 128 * t, 128)].astype(F32)
            b = or_ref[j, :, 128 * t : 128 * t + 128].astype(F32)
            tiles.append(pltpu.roll(a + b, turn, 1))
        for t in range(7):
            out_ref[slot, half, QROWS + 64 * t : QROWS + 64 * t + 64, :] = jnp.where(
                lane < 128 - shift, tiles[t], tiles[t + 1]
            )
        last = tiles[7]
        rest = last[0:16]
        for g in range(1, 4):
            rest = jnp.where(lane16 < 32 * g, rest, pltpu.roll(last[16 * g : 16 * g + 16], 32 * g, 1))
        out_ref[slot, half, QROWS + 448 : QROWS + 464, :] = rest
        return carry

    lax.fori_loop(0, 8, block, 0)


def table_pack_kernel(t_ref, out_ref):
    lane = lanes(64)
    for d in range(16):
        half, xb, core = d // 8, (d // 2) % 4, d % 2
        for i in range(2):
            first = 232 * d + 128 * i
            tile, shift = first // 128, first % 128
            v = t_ref[:, 128 * tile : 128 * tile + 128]
            if shift:
                v = pltpu.roll(v, 128 - shift, 1)
                if tile + 1 < 29:
                    w = pltpu.roll(t_ref[:, 128 * tile + 128 : 128 * tile + 256], 128 - shift, 1)
                    v = jnp.where(lane < 128 - shift, v, w)
            if i == 1:
                v = jnp.where(lane < 104, v, 0.0)
            out_ref[core, xb, half, 64 * i : 64 * i + 64, :] = v


def adamw(gradient, master, first, second, factor):
    clipped = gradient * factor
    first_new = beta_first * first + (1.0 - beta_first) * clipped
    second_new = beta_second * second + (1.0 - beta_second) * clipped * clipped
    first_hat = first_new / (1.0 - beta_first**STEP)
    second_hat = second_new / (1.0 - beta_second**STEP)
    master_new = master - learn_rate * (
        first_hat / (jnp.sqrt(second_hat) + tiny_value) + weight_decay * master
    )
    return master_new, first_new, second_new


def update_kernel(limit):
    def kernel(
        n_ref, g_ref, gt_ref,
        qw_ref, qm_ref, qv_ref, ow_ref, om_ref, ov_ref, tw_ref, tm_ref, tv_ref,
        pack_ref, tpack_ref,
        qw2_ref, qm2_ref, qv2_ref, ow2_ref, om2_ref, ov2_ref, tw2_ref, tm2_ref, tv2_ref,
    ):
        grad_norm = jnp.sqrt(jnp.sum(n_ref[...], keepdims=True))
        factor = jnp.minimum(1.0, limit / (grad_norm + 1e-06))

        def step(g, rows, cols, refs, outs):
            new = adamw(g, *(r[rows, cols] for r in refs), factor)
            for ref, value in zip(outs, new):
                ref[rows, cols] = value
            return new[0]

        refs, outs = (qw_ref, qm_ref, qv_ref), (qw2_ref, qm2_ref, qv2_ref)
        every = slice(None)
        new = [
            step(g_ref[8 * t : 8 * t + 8, :], every, slice(128 * t, 128 * t + 128), refs, outs)
            for t in range(QT)
        ]
        new.append(jnp.zeros_like(new[0]))
        for t in range(16):
            pack_ref[16 * t : 16 * t + 16, :] = jnp.concatenate(
                [new[t], new[t + 16]], axis=0
            ).astype(BF16)

        refs, outs = (ow_ref, om_ref, ov_ref), (ow2_ref, om2_ref, ov2_ref)
        for t in range(7):
            g = g_ref[QROWS + 64 * t : QROWS + 64 * t + 64, :]
            w = step(g, every, slice(128 * t, 128 * t + 128), refs, outs)
            pack_ref[WQ + 64 * t : WQ + 64 * t + 64, :] = w.astype(BF16)
        rest = g_ref[QROWS + 448 : QROWS + 464, :]
        lane = lanes(16)
        packed = jnp.zeros((16, 128), F32)
        for g in range(4):
            piece = rest if g == 0 else pltpu.roll(rest, 128 - 32 * g, 1)
            w = step(piece[:, 0:32], slice(16 * g, 16 * g + 16), slice(896, 928), refs, outs)
            w = jnp.concatenate([w, jnp.zeros((16, 96), F32)], axis=1)
            w = w if g == 0 else pltpu.roll(w, 32 * g, 1)
            packed = jnp.where((lane >= 32 * g) & (lane < 32 * g + 32), w, packed)
        pack_ref[WQ + 448 : WQ + 464, :] = packed.astype(BF16)

        refs, outs = (tw_ref, tm_ref, tv_ref), (tw2_ref, tm2_ref, tv2_ref)
        w = step(gt_ref[0:64, :], every, slice(0, 128), refs, outs)
        tpack_ref[0:64, :] = w.astype(BF16)
        w = step(gt_ref[64:128, 0:104], every, slice(128, 232), refs, outs)
        tpack_ref[64:128, :] = jnp.concatenate([w, jnp.zeros((64, 24), F32)], axis=1).astype(BF16)

    return kernel


def take(own_ref, got_ref, index, rows, mine):
    a = own_ref[(*index, rows, slice(None))].astype(F32)
    b = got_ref[(*index, rows, slice(None))].astype(F32)
    return jnp.where(mine, a, b)


def cover(t, width, count):
    found = []
    for b in range(count):
        begin = 128 * t - width * b
        for i in range(-(-width // 128)):
            lo = max(0, 128 * i - begin)
            hi = min(128, 128 * i - begin + 128, width - begin)
            if lo < hi:
                found.append((b, i, (-begin) % 128, lo, hi))
    return found


def join_kernel(own_ref, got_ref, q_ref, o_ref):
    zh, x, core = position()

    def rows(j, carry):
        index = ((x - j % 4 + 4) % 4, jnp.where(zh == j // 4, 0, 1))
        for p in range(16):
            a = own_ref[(*index, slice(16 * p, 16 * p + 16), slice(None))].astype(F32)
            b = got_ref[(*index, slice(16 * p, 16 * p + 16), slice(None))].astype(F32)
            c0, c1 = jnp.where(core == 0, a, b), jnp.where(core == 0, b, a)
            for t, part in ((p, slice(0, 8)), (p + 16, slice(8, 16))):
                if t < QT:
                    q_ref[pl.ds(pl.multiple_of(j * 16, 16), 16), 128 * t : 128 * t + 128] = (
                        jnp.concatenate([c0[part], c1[part]], axis=0).astype(BF16)
                    )
        return carry

    lax.fori_loop(0, 8, rows, 0)
    lane = lanes(64)

    def cols(g, carry):
        index = [
            ((x - (2 * (g % 2) + b // 2) + 4) % 4, jnp.where(zh == g // 2, 0, 1)) for b in range(4)
        ]

        def tile(b, i, turn):
            mine = core == b % 2
            if i < 7:
                v = take(own_ref, got_ref, index[b], slice(WQ + 64 * i, WQ + 64 * i + 64), mine)
                return pltpu.roll(v, turn, 1) if turn else v
            v = take(own_ref, got_ref, index[b], slice(WQ + 448, WQ + 464), mine)
            parts = []
            for k in range(4):
                move = (turn - 32 * k) % 128
                parts.append(pltpu.roll(v, move, 1) if move else v)
            return jnp.concatenate(parts, axis=0)

        base = pl.multiple_of(g * 3712, 128)
        for t in range(29):
            value = None
            for b, i, turn, lo, hi in cover(t, 928, 4):
                v = tile(b, i, turn)
                value = v if value is None else jnp.where(lane >= lo, v, value)
            o_ref[:, pl.ds(base + 128 * t, 128)] = value.astype(BF16)
        return carry

    lax.fori_loop(0, 4, cols, 0)


def table_join_kernel(own_ref, got_ref, t_ref):
    zh, x, core = position()
    section = lax.axis_index("section")
    lane = lanes(64)

    def quarter(s, carry):
        m = (section - s + 4) % 4
        base = pl.multiple_of(s * 3712, 128)
        for t in range(29):
            value = None
            for d, i, turn, lo, hi in cover(t, 232, 16):
                index = (m, (x - (d // 2) % 4 + 4) % 4, jnp.where(zh == d // 8, 0, 1))
                v = take(own_ref, got_ref, index, slice(64 * i, 64 * i + 64), core == d % 2)
                v = pltpu.roll(v, turn, 1) if turn else v
                value = v if value is None else jnp.where(lane >= lo, v, value)
            t_ref[:, pl.ds(base + 128 * t, 128)] = value.astype(BF16)
        return carry

    lax.fori_loop(0, 4, quarter, 0)


def per_device(
    query_grads,
    query_master,
    query_first,
    query_second,
    output_grads,
    output_master,
    output_first,
    output_second,
    table_grads,
    table_master,
    table_first,
    table_second,
):
    section = lax.axis_index("section")
    member = lax.axis_index("dp")
    zh, x, core = member // 8, (member // 2) % 4, member % 2
    query, output, table = query_grads[0, 0], output_grads[0, 0], table_grads[0, 0]

    def dp_send(value, perm):
        return lax.ppermute(value, "dp", perm)

    def quarter(i):
        return lax.dynamic_slice(table, (0, i * 3712), (64, 3712))

    first_section = section == 0
    at_ends = jnp.logical_or(first_section, section == 3)
    t_far = lax.ppermute(quarter(jnp.where(first_section, 2, 1)), "section", [(0, 2), (3, 1)])
    t_near = lax.ppermute(quarter(jnp.where(first_section, 1, 2)), "section", [(0, 1), (3, 2)])
    t_end = lax.ppermute(quarter(jnp.where(first_section, 3, 0)), "section", [(0, 3), (3, 0)])

    q_send, o_send = call(
        split_kernel, (out((64, 3968), BF16), out((8, 64, 1024), BF16)), query, output
    )
    q_got, o_got = dp_send(q_send, CORE), dp_send(o_send, CORE)
    sums = call(pack_kernel, out((4, 2, SUMS, 128), F32), query, output, q_got, o_got)

    got = [dp_send(sums[k].astype(F16), x_perm(k)) for k in (1, 2, 3)]
    total = sums[0] + got[0].astype(F32) + got[1].astype(F32) + got[2].astype(F32)
    z_got = dp_send(lax.dynamic_index_in_dim(total, 1 - zh, 0, False).astype(F16), ZHALF)
    gradient = lax.dynamic_index_in_dim(total, zh, 0, False) + z_got.astype(F32)

    t_sum = jnp.where(at_ends, quarter(section), t_near).astype(F32) + jnp.where(
        at_ends, t_end, t_far
    ).astype(F32)
    t_blocks = call(table_pack_kernel, out((2, 4, 2, TROWS, 128), F32), t_sum)
    t_got = dp_send(lax.dynamic_index_in_dim(t_blocks, 1 - core, 0, False).astype(F16), CORE)
    t_chip = lax.dynamic_index_in_dim(t_blocks, core, 0, False) + t_got.astype(F32)

    def t_slot(k):
        return lax.dynamic_index_in_dim(t_chip, (x + k) % 4, 0, False)

    t_gots = [dp_send(t_slot(k).astype(F16), x_perm(k)) for k in (1, 2, 3)]
    t_total = (
        t_slot(0) + t_gots[0].astype(F32) + t_gots[1].astype(F32) + t_gots[2].astype(F32)
    )
    tz_got = dp_send(lax.dynamic_index_in_dim(t_total, 1 - zh, 0, False).astype(F16), ZHALF)
    t_gradient = lax.dynamic_index_in_dim(t_total, zh, 0, False) + tz_got.astype(F32)

    squares = jnp.sum((gradient * gradient).reshape(-1, 8, 128), axis=0) + jnp.sum(
        (t_gradient * t_gradient).reshape(-1, 8, 128), axis=0
    )
    squares = squares + dp_send(squares, CORE)
    squares = squares + sum(dp_send(squares, x_perm(k)) for k in (1, 2, 3))
    squares = squares + sum(lax.ppermute(squares, "section", ring_perm(k)) for k in (1, 2, 3))
    squares = squares + dp_send(squares, ZHALF)
    squares = squares + sum(lax.ppermute(squares, "tensor", ring_perm(k)) for k in (1, 2, 3))

    params_count = 4 * (128 * 15872 + 256 * 14848) + 256 * 14848
    limit = 0.5 * math.sqrt(params_count)
    small = [out((8, 3968), F32)] * 3 + [out((64, 928), F32)] * 3 + [out((64, 232), F32)] * 3
    packed, t_packed, *new = call(
        update_kernel(limit),
        (out((WEIGHTS, 128), BF16), out((TROWS, 128), BF16), *small),
        squares, gradient, t_gradient,
        query_master[0], query_first[0], query_second[0],
        output_master[0], output_first[0], output_second[0],
        table_master, table_first, table_second,
    )

    def spread(value):
        both = jnp.stack([value, dp_send(value, ZHALF)])
        return jnp.stack([both] + [dp_send(both, x_perm(k)) for k in (1, 2, 3)])

    t_all = spread(t_packed)
    t_all = jnp.stack([t_all] + [lax.ppermute(t_all, "section", ring_perm(k)) for k in (1, 2, 3)])
    w_all = spread(packed)
    w_other = dp_send(w_all, CORE)
    t_other = dp_send(t_all, CORE)
    query_full, output_full = call(
        join_kernel, (out((128, 3968), BF16), out((64, 14848), BF16)), w_all, w_other
    )
    table_full = call(table_join_kernel, out((64, 14848), BF16), t_all, t_other)
    return (
        query_full[None],
        *(a[None] for a in new[0:3]),
        output_full[None],
        *(a[None] for a in new[3:6]),
        table_full,
        *new[6:9],
    )


def solution(mesh):
    return jax.shard_map(
        per_device,
        mesh=mesh,
        in_specs=(
            P("section", "dp", None, "tensor"),
            P("section", "dp", "tensor"),
            P("section", "dp", "tensor"),
            P("section", "dp", "tensor"),
            P("section", "dp", "tensor", None),
            P("section", "tensor", "dp"),
            P("section", "tensor", "dp"),
            P("section", "tensor", "dp"),
            P("section", "dp", "tensor", None),
            P("tensor", ("section", "dp")),
            P("tensor", ("section", "dp")),
            P("tensor", ("section", "dp")),
        ),
        out_specs=(
            P("section", None, "tensor"),
            P("section", "dp", "tensor"),
            P("section", "dp", "tensor"),
            P("section", "dp", "tensor"),
            P("section", "tensor", None),
            P("section", "tensor", "dp"),
            P("section", "tensor", "dp"),
            P("section", "tensor", "dp"),
            P("tensor", None),
            P("tensor", ("section", "dp")),
            P("tensor", ("section", "dp")),
            P("tensor", ("section", "dp")),
        ),
        check_vma=False,
    )
```

```python
import math

import jax
import jax.numpy as jnp
from jax import lax
from jax.experimental import pallas as pl
from jax.experimental.pallas import tpu as pltpu
from jax.sharding import PartitionSpec as P

STEP = 10

beta_first = 0.9
beta_second = 0.95
learn_rate = 0.02
weight_decay = 0.1
tiny_value = 1e-08

F32, BF16, F16 = jnp.float32, jnp.bfloat16, jnp.float16

QT = 31
QROWS, OROWS, TROWS = 256, 464, 128
PACK = QROWS + OROWS
UPPER = 352


def pair_perm(move):
    return [(d, move(d)) for d in range(16)]


CORE = pair_perm(lambda d: d ^ 1)
ZHALF = pair_perm(lambda d: d ^ 8)


def x_perm(e):
    return pair_perm(lambda d: d ^ (2 * e))


def ring_perm(k):
    return [(i, (i + k) % 4) for i in range(4)]


def lanes(rows):
    return lax.broadcasted_iota(jnp.int32, (rows, 128), 1)


def call(kernel, outs, *args, micros=2, hbm=(), out_hbm=(), scratch=(), vmem=16):
    return pl.pallas_call(
        kernel,
        out_shape=list(outs) if isinstance(outs, (list, tuple)) else outs,
        cost_estimate=pl.CostEstimate(flops=0, bytes_accessed=3000000 * micros, transcendentals=0),
        in_specs=[
            pl.BlockSpec(memory_space=pltpu.HBM if i in hbm else pltpu.VMEM)
            for i in range(len(args))
        ],
        out_specs=jax.tree.map(
            lambda i: pl.BlockSpec(memory_space=pltpu.HBM if i in out_hbm else pltpu.VMEM),
            list(range(len(outs))) if isinstance(outs, (list, tuple)) else 0,
        ),
        scratch_shapes=scratch,
        compiler_params=pltpu.CompilerParams(vmem_limit_bytes=vmem * 1024 * 1024),
    )(*args)


def out(shape, dtype):
    return jax.ShapeDtypeStruct(shape, dtype)


def position():
    d = lax.axis_index("dp")
    return d // 8, (d // 2) % 4, d % 2


def chunk_copy(src_ref, dst_ref, sems, index, chunk):
    return pltpu.make_async_copy(src_ref.at[chunk], dst_ref.at[chunk], sems.at[index])


def columns(s):
    return slice(None), pl.ds(pl.multiple_of(s * 3712, 128), 3712)


def rolled(value, turn):
    return pltpu.roll(value, turn, 1) if turn else value


def table_split_kernel(t_hbm, _, own_ref, send_ref, t_ref, sems):
    _, _, core = position()
    lane = lanes(64)
    for s in range(4):
        chunk_copy(t_hbm, t_ref, sems, s, columns(s)).start()

    def split(outs):
        def quarter(s, carry):
            chunk_copy(t_hbm, t_ref, sems, s, columns(s)).wait()
            base = pl.multiple_of(s * 3712, 128)
            for d in range(16):
                start, shift = 232 * d // 128, 232 * d % 128
                count = -(-(shift + 232) // 128)
                tiles = [
                    rolled(t_ref[:, pl.ds(base + 128 * (start + i), 128)], -shift % 128)
                    for i in range(count)
                ]
                for i in range(2):
                    v = tiles[i]
                    if shift and i + 1 < count:
                        v = jnp.where(lane < 128 - shift, v, tiles[i + 1])
                    if i == 1:
                        v = jnp.where(lane < 104, v, jnp.zeros_like(v))
                    outs[d % 2][s, d // 2, 64 * i : 64 * i + 64, :] = v
            return carry

        lax.fori_loop(0, 4, quarter, 0)

    pl.when(core == 0)(lambda: split((own_ref, send_ref)))
    pl.when(core == 1)(lambda: split((send_ref, own_ref)))


def split_kernel(q_hbm, o_hbm, own_ref, send_ref, tick_ref, q_ref, o_ref, q_sems, o_sems):
    _, x, core = position()
    lane = lanes(64)
    lane16 = lanes(16)

    def rows(s):
        return pl.ds(pl.multiple_of(s * 32, 32), 32), slice(None)

    tick_ref[...] = jnp.zeros_like(tick_ref)
    for s in range(4):
        chunk_copy(q_hbm, q_ref, q_sems, s, rows(s)).start()
        chunk_copy(o_hbm, o_ref, o_sems, s, columns(s)).start()

    def split(outs):
        def group(s, carry):
            chunk_copy(q_hbm, q_ref, q_sems, s, rows(s)).wait()
            chunk_copy(o_hbm, o_ref, o_sems, s, columns(s)).wait()
            half = s // 2
            for p in range(2):
                slot = (2 * (s % 2) + p) ^ x
                v = q_ref[pl.ds(pl.multiple_of(s * 32 + 16 * p, 16), 16), :]
                for c in range(2):
                    out_ref = outs[c]
                    part = v[8 * c : 8 * c + 8]
                    for t in range(16):
                        low = part[:, 128 * t : 128 * t + 128]
                        t2 = t + 16
                        high = part[:, 128 * t2 : 128 * t2 + 128] if t2 < QT else jnp.zeros_like(low)
                        out_ref[half, slot, 16 * t : 16 * t + 16, :] = jnp.concatenate(
                            [low, high], axis=0
                        )
                    b = 2 * p + c
                    shift = 32 * b
                    base = s * 3712 + 128 * (29 * b // 4)
                    tiles = [
                        rolled(
                            o_ref[:, pl.ds(pl.multiple_of(base + 128 * t, 128), 128)],
                            -shift % 128,
                        )
                        for t in range(8)
                    ]
                    for t in range(7):
                        w = jnp.where(lane < 128 - shift, tiles[t], tiles[t + 1]) if b else tiles[t]
                        first = QROWS + 64 * t
                        out_ref[half, slot, first : first + 64, :] = w
                    last = tiles[7]
                    rest = last[0:16]
                    for g in range(1, 4):
                        piece = pltpu.roll(last[16 * g : 16 * g + 16], 32 * g, 1)
                        rest = jnp.where(lane16 < 32 * g, rest, piece)
                    out_ref[half, slot, QROWS + 448 : QROWS + 464, :] = rest
            return carry

        lax.fori_loop(0, 4, group, 0)

    pl.when(core == 0)(lambda: split((own_ref, send_ref)))
    pl.when(core == 1)(lambda: split((send_ref, own_ref)))


def adamw(gradient, master, first, second, factor):
    clipped = gradient * factor
    first_new = beta_first * first + (1.0 - beta_first) * clipped
    second_new = beta_second * second + (1.0 - beta_second) * clipped * clipped
    first_hat = first_new / (1.0 - beta_first**STEP)
    second_hat = second_new / (1.0 - beta_second**STEP)
    master_new = master - learn_rate * (
        first_hat / (jnp.sqrt(second_hat) + tiny_value) + weight_decay * master
    )
    return master_new, first_new, second_new


def update_kernel(limit):
    def kernel(
        n_ref, g_ref,
        qw_ref, qm_ref, qv_ref, ow_ref, om_ref, ov_ref, tw_ref, tm_ref, tv_ref,
        pack_ref,
        qw2_ref, qm2_ref, qv2_ref, ow2_ref, om2_ref, ov2_ref, tw2_ref, tm2_ref, tv2_ref,
    ):
        grad_norm = jnp.sqrt(jnp.sum(n_ref[...], keepdims=True))
        factor = jnp.minimum(1.0, limit / (grad_norm + 1e-06))

        def step(g, rows, cols, refs, outs):
            new = adamw(g, *(r[rows, cols] for r in refs), factor)
            for ref, value in zip(outs, new):
                ref[rows, cols] = value
            return new[0]

        refs, outs = (qw_ref, qm_ref, qv_ref), (qw2_ref, qm2_ref, qv2_ref)
        every = slice(None)
        new = [
            step(
                g_ref[16 * (t % 16) + 8 * (t // 16) : 16 * (t % 16) + 8 * (t // 16) + 8, :],
                every, slice(128 * t, 128 * t + 128), refs, outs,
            )
            for t in range(QT)
        ]
        new.append(jnp.zeros_like(new[0]))
        for t in range(16):
            pack_ref[16 * t : 16 * t + 16, :] = jnp.concatenate(
                [new[t], new[t + 16]], axis=0
            ).astype(BF16)

        refs, outs = (ow_ref, om_ref, ov_ref), (ow2_ref, om2_ref, ov2_ref)
        for t in range(7):
            g = g_ref[QROWS + 64 * t : QROWS + 64 * t + 64, :]
            w = step(g, every, slice(128 * t, 128 * t + 128), refs, outs)
            pack_ref[QROWS + 64 * t : QROWS + 64 * t + 64, :] = w.astype(BF16)
        rest = g_ref[QROWS + 448 : QROWS + 464, :]
        lane = lanes(16)
        packed = jnp.zeros((16, 128), F32)
        for g in range(4):
            piece = rest if g == 0 else pltpu.roll(rest, 128 - 32 * g, 1)
            w = step(piece[:, 0:32], slice(16 * g, 16 * g + 16), slice(896, 928), refs, outs)
            w = jnp.concatenate([w, jnp.zeros((16, 96), F32)], axis=1)
            w = w if g == 0 else pltpu.roll(w, 32 * g, 1)
            packed = jnp.where((lane >= 32 * g) & (lane < 32 * g + 32), w, packed)
        pack_ref[QROWS + 448 : QROWS + 464, :] = packed.astype(BF16)

        refs, outs = (tw_ref, tm_ref, tv_ref), (tw2_ref, tm2_ref, tv2_ref)
        w = step(g_ref[PACK : PACK + 64, :], every, slice(0, 128), refs, outs)
        pack_ref[PACK : PACK + 64, :] = w.astype(BF16)
        w = step(g_ref[PACK + 64 : PACK + 128, 0:104], every, slice(128, 232), refs, outs)
        pack_ref[PACK + 64 : PACK + 128, :] = jnp.concatenate([w, jnp.zeros((64, 24), F32)], axis=1).astype(BF16)

    return kernel


def cover(t, width, count):
    found = []
    for b in range(count):
        begin = 128 * t - width * b
        for i in range(-(-width // 128)):
            lo = max(0, 128 * i - begin)
            hi = min(128, 128 * i - begin + 128, width - begin)
            if lo < hi:
                found.append((b, i, (-begin) % 128, lo, hi))
    return found


def join_kernel(own_ref, got_ref, _, q_hbm, o_hbm, q_ref, o_ref, q_sems, o_sems):
    zh, x, core = position()
    lane = lanes(64)

    def row_copy(j):
        chunk = pl.ds(pl.multiple_of(j * 16, 16), 16), slice(None)
        return chunk_copy(q_ref, q_hbm, q_sems, j, chunk)

    def join(refs):
        def rows(j, carry):
            index = (zh ^ (j // 4), x ^ (j % 4))
            for p in range(16):
                a, b = (ref[(*index, slice(16 * p, 16 * p + 16), slice(None))] for ref in refs)
                for t, part in ((p, slice(0, 8)), (p + 16, slice(8, 16))):
                    if t < QT:
                        q_ref[pl.ds(pl.multiple_of(j * 16, 16), 16), 128 * t : 128 * t + 128] = (
                            jnp.concatenate([a[part], b[part]], axis=0)
                        )
            row_copy(j).start()
            return carry

        lax.fori_loop(0, 8, rows, 0)

        def cols(g, carry):
            index = [
                (zh ^ (g // 2), x ^ (2 * (g % 2) + b // 2))
                for b in range(4)
            ]

            def tile(b, i, turn):
                if i < 7:
                    rows = slice(QROWS + 64 * i, QROWS + 64 * i + 64)
                    v = refs[b % 2][(*index[b], rows, slice(None))]
                    return pltpu.roll(v, turn, 1) if turn else v
                v = refs[b % 2][(*index[b], slice(QROWS + 448, QROWS + 464), slice(None))]
                parts = []
                for k in range(4):
                    move = (turn - 32 * k) % 128
                    parts.append(pltpu.roll(v, move, 1) if move else v)
                return jnp.concatenate(parts, axis=0)

            base = pl.multiple_of(g * 3712, 128)
            for t in range(29):
                value = None
                for b, i, turn, lo, hi in cover(t, 928, 4):
                    v = tile(b, i, turn)
                    value = v if value is None else jnp.where(lane >= lo, v, value)
                o_ref[:, pl.ds(base + 128 * t, 128)] = value
            chunk_copy(o_ref, o_hbm, o_sems, g, columns(g)).start()
            return carry

        lax.fori_loop(0, 4, cols, 0)

    pl.when(core == 0)(lambda: join((own_ref, got_ref)))
    pl.when(core == 1)(lambda: join((got_ref, own_ref)))
    for j in range(8):
        row_copy(j).wait()
    for g in range(4):
        chunk_copy(o_ref, o_hbm, o_sems, g, columns(g)).wait()


def table_join_kernel(own_ref, got_ref, t_hbm, tick_ref, t_ref, sems):
    tick_ref[...] = jnp.zeros_like(tick_ref)
    zh, x, core = position()
    section = lax.axis_index("section")
    lane = lanes(64)

    def join(refs):
        def quarter(s, carry):
            m = (section - s + 4) % 4
            base = pl.multiple_of(s * 3712, 128)
            for t in range(29):
                value = None
                for d, i, turn, lo, hi in cover(t, 232, 16):
                    index = (m, x ^ ((d // 2) % 4), zh ^ (d // 8))
                    rows = slice(64 * i, 64 * i + 64)
                    v = refs[d % 2][(*index, rows, slice(None))]
                    v = pltpu.roll(v, turn, 1) if turn else v
                    value = v if value is None else jnp.where(lane >= lo, v, value)
                t_ref[:, pl.ds(base + 128 * t, 128)] = value
            chunk_copy(t_ref, t_hbm, sems, s, columns(s)).start()
            return carry

        lax.fori_loop(0, 4, quarter, 0)

    pl.when(core == 0)(lambda: join((own_ref, got_ref)))
    pl.when(core == 1)(lambda: join((got_ref, own_ref)))
    for s in range(4):
        chunk_copy(t_ref, t_hbm, sems, s, columns(s)).wait()


def per_device(
    query_grads,
    query_master,
    query_first,
    query_second,
    output_grads,
    output_master,
    output_first,
    output_second,
    table_grads,
    table_master,
    table_first,
    table_second,
):
    section = lax.axis_index("section")
    member = lax.axis_index("dp")
    zh, x = member // 8, (member // 2) % 4
    query, output, table = query_grads[0, 0], output_grads[0, 0], table_grads[0, 0]

    def dp_send(value, perm):
        return lax.ppermute(value, "dp", perm)

    def pick(value, i):
        return lax.dynamic_index_in_dim(value, i, 0, False)

    own, send, tick = call(
        split_kernel, [out((2, 4, PACK, 128), BF16)] * 2 + [out((8, 128), F32)], query, output,
        hbm=(0, 1), micros=3, vmem=60,
        scratch=[
            pltpu.VMEM((128, 3968), BF16), pltpu.VMEM((64, 14848), BF16),
            pltpu.SemaphoreType.DMA((4,)), pltpu.SemaphoreType.DMA((4,)),
        ],
    )
    got = dp_send(send, CORE)
    t_own, t_send = call(
        table_split_kernel, [out((4, 8, TROWS, 128), BF16)] * 2, table, tick, hbm=(0,),
        scratch=[pltpu.VMEM((64, 14848), BF16), pltpu.SemaphoreType.DMA((4,))],
    )

    def slots(h, e):
        return own[h, e].astype(F32) + got[h, e].astype(F32)

    near, wrap = slots(0, slice(1, 3)).astype(F16), slots(1, slice(2, 4)).astype(F16)
    near, wrap, t_send = lax.optimization_barrier((near, wrap, t_send))
    t_got = dp_send(t_send, CORE)
    near = dp_send(near, x_perm(1)).astype(F32)
    wrap = dp_send(wrap, x_perm(3)).astype(F32)
    near_last = dp_send((slots(0, 3) + near[1]).astype(F16), x_perm(3)).astype(F32)
    wrap_last = dp_send((slots(1, 1) + wrap[0]).astype(F16), x_perm(1)).astype(F32)
    halves = (slots(0, 0) + near[0] + near_last, slots(1, 0) + wrap[1] + wrap_last)

    first_section = section == 0
    at_ends = jnp.logical_or(first_section, section == 3)

    def quarter(i):
        return pick(t_own, i).astype(F32) + pick(t_got, i).astype(F32)

    def section_send(i, perm):
        return lax.ppermute(quarter(i).astype(F16), "section", perm)

    t_far = section_send(jnp.where(first_section, 2, 1), [(0, 2), (3, 1)])
    t_near = section_send(jnp.where(first_section, 1, 2), [(0, 1), (3, 2)])
    t_end = section_send(jnp.where(first_section, 3, 0), [(0, 3), (3, 0)])
    t_sum = jnp.where(at_ends, quarter(section), t_near.astype(F32)) + jnp.where(
        at_ends, t_end, t_far
    ).astype(F32)
    t_sum = t_sum.reshape(2, 4, TROWS, 128)

    def t_slot(k):
        return lax.dynamic_index_in_dim(t_sum, x ^ k, 1, False)

    t_parts = [t_slot(0)] + [dp_send(t_slot(k).astype(F16), x_perm(k)) for k in (1, 2, 3)]

    first_half = zh == 0

    def t_half(i):
        return sum(pick(v, i).astype(F32) for v in t_parts)

    leave = jnp.concatenate([jnp.where(first_half, halves[1], halves[0]), t_half(1 - zh)])
    keep = jnp.concatenate([jnp.where(first_half, halves[0], halves[1]), t_half(zh)])
    gradient = keep + dp_send(leave.astype(F16), ZHALF).astype(F32)

    squares = jnp.sum((gradient * gradient).reshape(-1, 8, 128), axis=0)
    squares = squares + dp_send(squares, CORE)
    squares = squares + sum(dp_send(squares, x_perm(k)) for k in (1, 2, 3))
    squares = squares + sum(lax.ppermute(squares, "section", ring_perm(k)) for k in (1, 2, 3))
    squares = squares + dp_send(squares, ZHALF)
    squares = squares + sum(lax.ppermute(squares, "tensor", ring_perm(k)) for k in (1, 2, 3))

    params_count = 4 * (128 * 15872 + 256 * 14848) + 256 * 14848
    limit = 0.5 * math.sqrt(params_count)
    small = [out((8, 3968), F32)] * 3 + [out((64, 928), F32)] * 3 + [out((64, 232), F32)] * 3
    packed, *new = call(
        update_kernel(limit),
        (out((PACK + TROWS, 128), BF16), *small),
        squares, gradient,
        query_master[0], query_first[0], query_second[0],
        output_master[0], output_first[0], output_second[0],
        table_master, table_first, table_second,
    )

    def along_x(value):
        return jnp.stack([value] + [dp_send(value, x_perm(k)) for k in (1, 2, 3)])

    packed = jnp.stack([packed, dp_send(packed, ZHALF)])
    t_all = along_x(packed[:, PACK:])
    upper, lower = packed[:, :UPPER], packed[:, UPPER:PACK]
    upper_wrap = dp_send(upper, x_perm(3))
    lower_near = dp_send(lower, x_perm(1))
    _, upper_wrap, lower_near = lax.optimization_barrier((t_all, upper_wrap, lower_near))
    t_all = jnp.stack([t_all] + [lax.ppermute(t_all, "section", ring_perm(k)) for k in (1, 2, 3)])
    upper_rest = dp_send(jnp.stack([upper, upper_wrap]), x_perm(1))
    lower_rest = dp_send(jnp.stack([lower, lower_near]), x_perm(3))
    _, upper_rest, lower_rest = lax.optimization_barrier((t_all, upper_rest, lower_rest))
    w_all = jnp.concatenate(
        [
            jnp.stack([upper, upper_rest[0], upper_rest[1], upper_wrap], axis=1),
            jnp.stack([lower, lower_near, lower_rest[1], lower_rest[0]], axis=1),
        ],
        axis=2,
    )
    t_other = dp_send(t_all, CORE)
    t_other, w_all = lax.optimization_barrier((t_other, w_all))
    w_other = dp_send(w_all, CORE)
    table_full, tick = call(
        table_join_kernel, (out((64, 14848), BF16), out((8, 128), F32)), t_all, t_other,
        out_hbm=(0,), scratch=[pltpu.VMEM((64, 14848), BF16), pltpu.SemaphoreType.DMA((4,))],
    )
    query_full, output_full = call(
        join_kernel, (out((128, 3968), BF16), out((64, 14848), BF16)),
        w_all, w_other, tick, micros=3, out_hbm=(0, 1),
        scratch=[
            pltpu.VMEM((128, 3968), BF16), pltpu.VMEM((64, 14848), BF16),
            pltpu.SemaphoreType.DMA((8,)), pltpu.SemaphoreType.DMA((4,)),
        ],
    )
    return (
        query_full[None],
        *(a[None] for a in new[0:3]),
        output_full[None],
        *(a[None] for a in new[3:6]),
        table_full,
        *new[6:9],
    )


def solution(mesh):
    return jax.shard_map(
        per_device,
        mesh=mesh,
        in_specs=(
            P("section", "dp", None, "tensor"),
            P("section", "dp", "tensor"),
            P("section", "dp", "tensor"),
            P("section", "dp", "tensor"),
            P("section", "dp", "tensor", None),
            P("section", "tensor", "dp"),
            P("section", "tensor", "dp"),
            P("section", "tensor", "dp"),
            P("section", "dp", "tensor", None),
            P("tensor", ("section", "dp")),
            P("tensor", ("section", "dp")),
            P("tensor", ("section", "dp")),
        ),
        out_specs=(
            P("section", None, "tensor"),
            P("section", "dp", "tensor"),
            P("section", "dp", "tensor"),
            P("section", "dp", "tensor"),
            P("section", "tensor", None),
            P("section", "tensor", "dp"),
            P("section", "tensor", "dp"),
            P("section", "tensor", "dp"),
            P("tensor", None),
            P("tensor", ("section", "dp")),
            P("tensor", ("section", "dp")),
            P("tensor", ("section", "dp")),
        ),
        check_vma=False,
    )
```

```python
import math

import jax
import jax.numpy as jnp
from jax import lax
from jax.experimental import pallas as pl
from jax.experimental.pallas import tpu as pltpu
from jax.sharding import PartitionSpec as P

STEP = 10

beta_first = 0.9
beta_second = 0.95
learn_rate = 0.02
weight_decay = 0.1
tiny_value = 1e-08

F32, BF16, F16 = jnp.float32, jnp.bfloat16, jnp.float16

QT = 31
QROWS, OROWS, TROWS = 256, 464, 128
PACK = QROWS + OROWS
UPPER = 352


def pair_perm(move):
    return [(d, move(d)) for d in range(16)]


CORE = pair_perm(lambda d: d ^ 1)
ZHALF = pair_perm(lambda d: d ^ 8)


def x_perm(e):
    return pair_perm(lambda d: d ^ (2 * e))


def ring_perm(k):
    return [(i, (i + k) % 4) for i in range(4)]


def lanes(rows):
    return lax.broadcasted_iota(jnp.int32, (rows, 128), 1)


def call(kernel, outs, *args, micros=2, hbm=(), out_hbm=(), scratch=(), vmem=16):
    return pl.pallas_call(
        kernel,
        out_shape=list(outs) if isinstance(outs, (list, tuple)) else outs,
        cost_estimate=pl.CostEstimate(flops=0, bytes_accessed=3000000 * micros, transcendentals=0),
        in_specs=[
            pl.BlockSpec(memory_space=pltpu.HBM if i in hbm else pltpu.VMEM)
            for i in range(len(args))
        ],
        out_specs=jax.tree.map(
            lambda i: pl.BlockSpec(memory_space=pltpu.HBM if i in out_hbm else pltpu.VMEM),
            list(range(len(outs))) if isinstance(outs, (list, tuple)) else 0,
        ),
        scratch_shapes=scratch,
        compiler_params=pltpu.CompilerParams(vmem_limit_bytes=vmem * 1024 * 1024),
    )(*args)


def out(shape, dtype):
    return jax.ShapeDtypeStruct(shape, dtype)


def position():
    d = lax.axis_index("dp")
    return d // 8, (d // 2) % 4, d % 2


def chunk_copy(src_ref, dst_ref, sems, index, chunk):
    return pltpu.make_async_copy(src_ref.at[chunk], dst_ref.at[chunk], sems.at[index])


def columns(s):
    return slice(None), pl.ds(pl.multiple_of(s * 3712, 128), 3712)


def rolled(value, turn):
    return pltpu.roll(value, turn, 1) if turn else value


def table_split_kernel(t_hbm, _, own_ref, send_ref, t_ref, sems):
    _, _, core = position()
    lane = lanes(64)
    for s in range(4):
        chunk_copy(t_hbm, t_ref, sems, s, columns(s)).start()

    def split(outs):
        def quarter(s, carry):
            chunk_copy(t_hbm, t_ref, sems, s, columns(s)).wait()
            base = pl.multiple_of(s * 3712, 128)
            for d in range(16):
                start, shift = 232 * d // 128, 232 * d % 128
                count = -(-(shift + 232) // 128)
                tiles = [
                    rolled(t_ref[:, pl.ds(base + 128 * (start + i), 128)], -shift % 128)
                    for i in range(count)
                ]
                for i in range(2):
                    v = tiles[i]
                    if shift and i + 1 < count:
                        v = jnp.where(lane < 128 - shift, v, tiles[i + 1])
                    if i == 1:
                        v = jnp.where(lane < 104, v, jnp.zeros_like(v))
                    outs[d % 2][s, d // 2, 64 * i : 64 * i + 64, :] = v
            return carry

        lax.fori_loop(0, 4, quarter, 0)

    pl.when(core == 0)(lambda: split((own_ref, send_ref)))
    pl.when(core == 1)(lambda: split((send_ref, own_ref)))


def split_kernel(q_hbm, o_hbm, own_ref, send_ref, tick_ref, q_ref, o_ref, q_sems, o_sems):
    _, x, core = position()
    lane = lanes(64)
    lane16 = lanes(16)

    def rows(s):
        return pl.ds(pl.multiple_of(s * 32, 32), 32), slice(None)

    tick_ref[...] = jnp.zeros_like(tick_ref)
    for s in range(4):
        chunk_copy(q_hbm, q_ref, q_sems, s, rows(s)).start()
        chunk_copy(o_hbm, o_ref, o_sems, s, columns(s)).start()

    def split(outs):
        def group(s, carry):
            chunk_copy(q_hbm, q_ref, q_sems, s, rows(s)).wait()
            chunk_copy(o_hbm, o_ref, o_sems, s, columns(s)).wait()
            half = s // 2
            for p in range(2):
                slot = (2 * (s % 2) + p) ^ x
                v = q_ref[pl.ds(pl.multiple_of(s * 32 + 16 * p, 16), 16), :]
                for c in range(2):
                    out_ref = outs[c]
                    part = v[8 * c : 8 * c + 8]
                    for t in range(16):
                        low = part[:, 128 * t : 128 * t + 128]
                        t2 = t + 16
                        high = part[:, 128 * t2 : 128 * t2 + 128] if t2 < QT else jnp.zeros_like(low)
                        out_ref[half, slot, 16 * t : 16 * t + 16, :] = jnp.concatenate(
                            [low, high], axis=0
                        )
                    b = 2 * p + c
                    shift = 32 * b
                    base = s * 3712 + 128 * (29 * b // 4)
                    tiles = [
                        rolled(
                            o_ref[:, pl.ds(pl.multiple_of(base + 128 * t, 128), 128)],
                            -shift % 128,
                        )
                        for t in range(8)
                    ]
                    for t in range(7):
                        w = jnp.where(lane < 128 - shift, tiles[t], tiles[t + 1]) if b else tiles[t]
                        first = QROWS + 64 * t
                        out_ref[half, slot, first : first + 64, :] = w
                    last = tiles[7]
                    rest = last[0:16]
                    for g in range(1, 4):
                        piece = pltpu.roll(last[16 * g : 16 * g + 16], 32 * g, 1)
                        rest = jnp.where(lane16 < 32 * g, rest, piece)
                    out_ref[half, slot, QROWS + 448 : QROWS + 464, :] = rest
            return carry

        lax.fori_loop(0, 4, group, 0)

    pl.when(core == 0)(lambda: split((own_ref, send_ref)))
    pl.when(core == 1)(lambda: split((send_ref, own_ref)))


def adamw(gradient, master, first, second, factor):
    clipped = gradient * factor
    first_new = beta_first * first + (1.0 - beta_first) * clipped
    second_new = beta_second * second + (1.0 - beta_second) * clipped * clipped
    first_hat = first_new / (1.0 - beta_first**STEP)
    second_hat = second_new / (1.0 - beta_second**STEP)
    master_new = master - learn_rate * (
        first_hat / (jnp.sqrt(second_hat) + tiny_value) + weight_decay * master
    )
    return master_new, first_new, second_new


def update_kernel(limit):
    def kernel(
        n_ref, g_ref,
        qw_ref, qm_ref, qv_ref, ow_ref, om_ref, ov_ref, tw_ref, tm_ref, tv_ref,
        pack_ref,
        qw2_ref, qm2_ref, qv2_ref, ow2_ref, om2_ref, ov2_ref, tw2_ref, tm2_ref, tv2_ref,
    ):
        grad_norm = jnp.sqrt(jnp.sum(n_ref[...], keepdims=True))
        factor = jnp.minimum(1.0, limit / (grad_norm + 1e-06))

        def step(g, rows, cols, refs, outs):
            new = adamw(g, *(r[rows, cols] for r in refs), factor)
            for ref, value in zip(outs, new):
                ref[rows, cols] = value
            return new[0]

        refs, outs = (qw_ref, qm_ref, qv_ref), (qw2_ref, qm2_ref, qv2_ref)
        every = slice(None)
        new = [
            step(
                g_ref[16 * (t % 16) + 8 * (t // 16) : 16 * (t % 16) + 8 * (t // 16) + 8, :],
                every, slice(128 * t, 128 * t + 128), refs, outs,
            )
            for t in range(QT)
        ]
        new.append(jnp.zeros_like(new[0]))
        for t in range(16):
            pack_ref[16 * t : 16 * t + 16, :] = jnp.concatenate(
                [new[t], new[t + 16]], axis=0
            ).astype(BF16)

        refs, outs = (ow_ref, om_ref, ov_ref), (ow2_ref, om2_ref, ov2_ref)
        for t in range(7):
            g = g_ref[QROWS + 64 * t : QROWS + 64 * t + 64, :]
            w = step(g, every, slice(128 * t, 128 * t + 128), refs, outs)
            pack_ref[QROWS + 64 * t : QROWS + 64 * t + 64, :] = w.astype(BF16)
        rest = g_ref[QROWS + 448 : QROWS + 464, :]
        lane = lanes(16)
        packed = jnp.zeros((16, 128), F32)
        for g in range(4):
            piece = rest if g == 0 else pltpu.roll(rest, 128 - 32 * g, 1)
            w = step(piece[:, 0:32], slice(16 * g, 16 * g + 16), slice(896, 928), refs, outs)
            w = jnp.concatenate([w, jnp.zeros((16, 96), F32)], axis=1)
            w = w if g == 0 else pltpu.roll(w, 32 * g, 1)
            packed = jnp.where((lane >= 32 * g) & (lane < 32 * g + 32), w, packed)
        pack_ref[QROWS + 448 : QROWS + 464, :] = packed.astype(BF16)

        refs, outs = (tw_ref, tm_ref, tv_ref), (tw2_ref, tm2_ref, tv2_ref)
        w = step(g_ref[PACK : PACK + 64, :], every, slice(0, 128), refs, outs)
        pack_ref[PACK : PACK + 64, :] = w.astype(BF16)
        w = step(g_ref[PACK + 64 : PACK + 128, 0:104], every, slice(128, 232), refs, outs)
        pack_ref[PACK + 64 : PACK + 128, :] = jnp.concatenate([w, jnp.zeros((64, 24), F32)], axis=1).astype(BF16)

    return kernel


def cover(t, width, count):
    found = []
    for b in range(count):
        begin = 128 * t - width * b
        for i in range(-(-width // 128)):
            lo = max(0, 128 * i - begin)
            hi = min(128, 128 * i - begin + 128, width - begin)
            if lo < hi:
                found.append((b, i, (-begin) % 128, lo, hi))
    return found


def join_kernel(own_ref, got_ref, q_hbm, o_hbm, tick_ref, q_ref, o_ref, q_sems, o_sems):
    tick_ref[...] = jnp.zeros_like(tick_ref)
    zh, x, core = position()
    lane = lanes(64)

    def row_copy(j):
        chunk = pl.ds(pl.multiple_of(j * 16, 16), 16), slice(None)
        return chunk_copy(q_ref, q_hbm, q_sems, j, chunk)

    def join(refs):
        def rows(j, carry):
            index = (zh ^ (j // 4), x ^ (j % 4))
            for p in range(16):
                a, b = (ref[(*index, slice(16 * p, 16 * p + 16), slice(None))] for ref in refs)
                for t, part in ((p, slice(0, 8)), (p + 16, slice(8, 16))):
                    if t < QT:
                        q_ref[pl.ds(pl.multiple_of(j * 16, 16), 16), 128 * t : 128 * t + 128] = (
                            jnp.concatenate([a[part], b[part]], axis=0)
                        )
            row_copy(j).start()
            return carry

        lax.fori_loop(0, 8, rows, 0)

        def cols(g, carry):
            index = [
                (zh ^ (g // 2), x ^ (2 * (g % 2) + b // 2))
                for b in range(4)
            ]

            def tile(b, i, turn):
                if i < 7:
                    rows = slice(QROWS + 64 * i, QROWS + 64 * i + 64)
                    v = refs[b % 2][(*index[b], rows, slice(None))]
                    return pltpu.roll(v, turn, 1) if turn else v
                v = refs[b % 2][(*index[b], slice(QROWS + 448, QROWS + 464), slice(None))]
                parts = []
                for k in range(4):
                    move = (turn - 32 * k) % 128
                    parts.append(pltpu.roll(v, move, 1) if move else v)
                return jnp.concatenate(parts, axis=0)

            base = pl.multiple_of(g * 3712, 128)
            for t in range(29):
                value = None
                for b, i, turn, lo, hi in cover(t, 928, 4):
                    v = tile(b, i, turn)
                    value = v if value is None else jnp.where(lane >= lo, v, value)
                o_ref[:, pl.ds(base + 128 * t, 128)] = value
            chunk_copy(o_ref, o_hbm, o_sems, g, columns(g)).start()
            return carry

        lax.fori_loop(0, 4, cols, 0)

    pl.when(core == 0)(lambda: join((own_ref, got_ref)))
    pl.when(core == 1)(lambda: join((got_ref, own_ref)))
    for j in range(8):
        row_copy(j).wait()
    for g in range(4):
        chunk_copy(o_ref, o_hbm, o_sems, g, columns(g)).wait()


def table_join_kernel(own_ref, got_ref, _, t_hbm, t_ref, sems):
    zh, x, core = position()
    section = lax.axis_index("section")
    lane = lanes(64)

    def join(refs):
        def quarter(s, carry):
            m = (section - s + 4) % 4
            base = pl.multiple_of(s * 3712, 128)
            for t in range(29):
                value = None
                for d, i, turn, lo, hi in cover(t, 232, 16):
                    index = (m, x ^ ((d // 2) % 4), zh ^ (d // 8))
                    rows = slice(64 * i, 64 * i + 64)
                    v = refs[d % 2][(*index, rows, slice(None))]
                    v = pltpu.roll(v, turn, 1) if turn else v
                    value = v if value is None else jnp.where(lane >= lo, v, value)
                t_ref[:, pl.ds(base + 128 * t, 128)] = value
            chunk_copy(t_ref, t_hbm, sems, s, columns(s)).start()
            return carry

        lax.fori_loop(0, 4, quarter, 0)

    pl.when(core == 0)(lambda: join((own_ref, got_ref)))
    pl.when(core == 1)(lambda: join((got_ref, own_ref)))
    for s in range(4):
        chunk_copy(t_ref, t_hbm, sems, s, columns(s)).wait()


def per_device(
    query_grads,
    query_master,
    query_first,
    query_second,
    output_grads,
    output_master,
    output_first,
    output_second,
    table_grads,
    table_master,
    table_first,
    table_second,
):
    section = lax.axis_index("section")
    member = lax.axis_index("dp")
    zh, x = member // 8, (member // 2) % 4
    query, output, table = query_grads[0, 0], output_grads[0, 0], table_grads[0, 0]

    def dp_send(value, perm):
        return lax.ppermute(value, "dp", perm)

    def pick(value, i):
        return lax.dynamic_index_in_dim(value, i, 0, False)

    own, send, tick = call(
        split_kernel, [out((2, 4, PACK, 128), BF16)] * 2 + [out((8, 128), F32)], query, output,
        hbm=(0, 1), micros=3, vmem=60,
        scratch=[
            pltpu.VMEM((128, 3968), BF16), pltpu.VMEM((64, 14848), BF16),
            pltpu.SemaphoreType.DMA((4,)), pltpu.SemaphoreType.DMA((4,)),
        ],
    )
    got = dp_send(send, CORE)
    t_own, t_send = call(
        table_split_kernel, [out((4, 8, TROWS, 128), BF16)] * 2, table, tick, hbm=(0,),
        scratch=[pltpu.VMEM((64, 14848), BF16), pltpu.SemaphoreType.DMA((4,))],
    )

    def slots(h, e):
        return own[h, e].astype(F32) + got[h, e].astype(F32)

    near, wrap = slots(0, slice(1, 3)).astype(F16), slots(1, slice(2, 4)).astype(F16)
    near, wrap, t_send = lax.optimization_barrier((near, wrap, t_send))
    t_got = dp_send(t_send, CORE)
    near = dp_send(near, x_perm(1))
    wrap = dp_send(wrap, x_perm(3))
    near_last = dp_send((slots(0, 3) + near[1].astype(F32)).astype(F16), x_perm(3)).astype(F32)
    wrap_last = dp_send((slots(1, 1) + wrap[0].astype(F32)).astype(F16), x_perm(1)).astype(F32)
    halves = (
        slots(0, 0) + near[0].astype(F32) + near_last,
        slots(1, 0) + wrap[1].astype(F32) + wrap_last,
    )

    first_section = section == 0
    at_ends = jnp.logical_or(first_section, section == 3)

    def quarter(i):
        return pick(t_own, i).astype(F32) + pick(t_got, i).astype(F32)

    def section_send(i, perm):
        return lax.ppermute(quarter(i).astype(F16), "section", perm)

    t_far = section_send(jnp.where(first_section, 2, 1), [(0, 2), (3, 1)])
    t_near = section_send(jnp.where(first_section, 1, 2), [(0, 1), (3, 2)])
    t_end = section_send(jnp.where(first_section, 3, 0), [(0, 3), (3, 0)])
    t_sum = jnp.where(at_ends, quarter(section), t_near.astype(F32)) + jnp.where(
        at_ends, t_end, t_far
    ).astype(F32)
    t_sum = t_sum.reshape(2, 4, TROWS, 128)

    def t_slot(k):
        return lax.dynamic_index_in_dim(t_sum, x ^ k, 1, False)

    t_parts = [t_slot(0)] + [dp_send(t_slot(k).astype(F16), x_perm(k)) for k in (1, 2, 3)]

    first_half = zh == 0

    def t_half(i):
        return sum(pick(v, i).astype(F32) for v in t_parts)

    leave = jnp.concatenate([jnp.where(first_half, halves[1], halves[0]), t_half(1 - zh)])
    keep = jnp.concatenate([jnp.where(first_half, halves[0], halves[1]), t_half(zh)])
    gradient = keep + dp_send(leave.astype(F16), ZHALF).astype(F32)

    squares = jnp.sum((gradient * gradient).reshape(-1, 8, 128), axis=0)
    squares = squares + dp_send(squares, CORE)
    squares = squares + sum(dp_send(squares, x_perm(k)) for k in (1, 2, 3))
    squares = squares + sum(lax.ppermute(squares, "section", ring_perm(k)) for k in (1, 2, 3))
    squares = squares + dp_send(squares, ZHALF)
    squares = squares + sum(lax.ppermute(squares, "tensor", ring_perm(k)) for k in (1, 2, 3))

    params_count = 4 * (128 * 15872 + 256 * 14848) + 256 * 14848
    limit = 0.5 * math.sqrt(params_count)
    small = [out((8, 3968), F32)] * 3 + [out((64, 928), F32)] * 3 + [out((64, 232), F32)] * 3
    packed, *new = call(
        update_kernel(limit),
        (out((PACK + TROWS, 128), BF16), *small),
        squares, gradient,
        query_master[0], query_first[0], query_second[0],
        output_master[0], output_first[0], output_second[0],
        table_master, table_first, table_second,
    )

    mine = [packed] + [dp_send(packed, x_perm(e)) for e in (1, 2, 3)]
    z_got = dp_send(packed, ZHALF)
    *mine, z_got = lax.optimization_barrier((*mine, z_got))

    t_got = z_got[PACK:]
    t_others = [t_got] + [dp_send(t_got, x_perm(e)) for e in (1, 2, 3)]
    upper, lower = z_got[:UPPER], z_got[UPPER:PACK]
    upper_wrap = dp_send(upper, x_perm(3))
    lower_near = dp_send(lower, x_perm(1))
    w_mine = jnp.stack([m[:PACK] for m in mine])
    mine_other = dp_send(w_mine, CORE)
    *_, mine_other, upper_wrap, lower_near = lax.optimization_barrier(
        (*t_others, mine_other, upper_wrap, lower_near)
    )
    t_all = jnp.stack([jnp.stack([m[PACK:], t]) for m, t in zip(mine, t_others)])
    t_all = jnp.stack([t_all] + [lax.ppermute(t_all, "section", ring_perm(k)) for k in (1, 2, 3)])
    upper_rest = dp_send(jnp.stack([upper, upper_wrap]), x_perm(1))
    lower_rest = dp_send(jnp.stack([lower, lower_near]), x_perm(3))
    _, upper_rest, lower_rest = lax.optimization_barrier((t_all, upper_rest, lower_rest))
    w_rest = jnp.concatenate(
        [
            jnp.stack([upper, upper_rest[0], upper_rest[1], upper_wrap]),
            jnp.stack([lower, lower_near, lower_rest[1], lower_rest[0]]),
        ],
        axis=1,
    )
    rest_other = dp_send(w_rest, CORE)
    t_other = dp_send(t_all, CORE)
    query_full, output_full, tick = call(
        join_kernel, (out((128, 3968), BF16), out((64, 14848), BF16), out((8, 128), F32)),
        jnp.stack([w_mine, w_rest]), jnp.stack([mine_other, rest_other]), micros=3, out_hbm=(0, 1),
        scratch=[
            pltpu.VMEM((128, 3968), BF16), pltpu.VMEM((64, 14848), BF16),
            pltpu.SemaphoreType.DMA((8,)), pltpu.SemaphoreType.DMA((4,)),
        ],
    )
    table_full = call(
        table_join_kernel, out((64, 14848), BF16), t_all, t_other, tick, out_hbm=(0,),
        scratch=[pltpu.VMEM((64, 14848), BF16), pltpu.SemaphoreType.DMA((4,))],
    )
    return (
        query_full[None],
        *(a[None] for a in new[0:3]),
        output_full[None],
        *(a[None] for a in new[3:6]),
        table_full,
        *new[6:9],
    )


def solution(mesh):
    return jax.shard_map(
        per_device,
        mesh=mesh,
        in_specs=(
            P("section", "dp", None, "tensor"),
            P("section", "dp", "tensor"),
            P("section", "dp", "tensor"),
            P("section", "dp", "tensor"),
            P("section", "dp", "tensor", None),
            P("section", "tensor", "dp"),
            P("section", "tensor", "dp"),
            P("section", "tensor", "dp"),
            P("section", "dp", "tensor", None),
            P("tensor", ("section", "dp")),
            P("tensor", ("section", "dp")),
            P("tensor", ("section", "dp")),
        ),
        out_specs=(
            P("section", None, "tensor"),
            P("section", "dp", "tensor"),
            P("section", "dp", "tensor"),
            P("section", "dp", "tensor"),
            P("section", "tensor", None),
            P("section", "tensor", "dp"),
            P("section", "tensor", "dp"),
            P("section", "tensor", "dp"),
            P("tensor", None),
            P("tensor", ("section", "dp")),
            P("tensor", ("section", "dp")),
            P("tensor", ("section", "dp")),
        ),
        check_vma=False,
    )
```

```python
import math

import jax
import jax.numpy as jnp
from jax import lax
from jax.experimental import pallas as pl
from jax.experimental.pallas import tpu as pltpu
from jax.sharding import PartitionSpec as P

STEP = 10

beta_first = 0.9
beta_second = 0.95
learn_rate = 0.02
weight_decay = 0.1
tiny_value = 1e-08

F32, BF16, F16 = jnp.float32, jnp.bfloat16, jnp.float16

QT = 31
QROWS, OROWS, TROWS = 256, 464, 128
PACK = QROWS + OROWS
UPPER = 352


def pair_perm(move):
    return [(d, move(d)) for d in range(16)]


CORE = pair_perm(lambda d: d ^ 1)
ZHALF = pair_perm(lambda d: d ^ 8)


def x_perm(e):
    return pair_perm(lambda d: d ^ (2 * e))


def line_perm(e):
    return [(i, i ^ e) for i in range(4)]


def ring_perm(k):
    return [(i, (i + k) % 4) for i in range(4)]


def lanes(rows):
    return lax.broadcasted_iota(jnp.int32, (rows, 128), 1)


def call(kernel, outs, *args, micros=2, hbm=(), out_hbm=(), scratch=(), vmem=16):
    return pl.pallas_call(
        kernel,
        out_shape=list(outs) if isinstance(outs, (list, tuple)) else outs,
        cost_estimate=pl.CostEstimate(flops=0, bytes_accessed=3000000 * micros, transcendentals=0),
        in_specs=[
            pl.BlockSpec(memory_space=pltpu.HBM if i in hbm else pltpu.VMEM)
            for i in range(len(args))
        ],
        out_specs=jax.tree.map(
            lambda i: pl.BlockSpec(memory_space=pltpu.HBM if i in out_hbm else pltpu.VMEM),
            list(range(len(outs))) if isinstance(outs, (list, tuple)) else 0,
        ),
        scratch_shapes=scratch,
        compiler_params=pltpu.CompilerParams(vmem_limit_bytes=vmem * 1024 * 1024),
    )(*args)


def out(shape, dtype):
    return jax.ShapeDtypeStruct(shape, dtype)


def position():
    d = lax.axis_index("dp")
    return d // 8, (d // 2) % 4, d % 2


def chunk_copy(src_ref, dst_ref, sems, index, chunk):
    return pltpu.make_async_copy(src_ref.at[chunk], dst_ref.at[chunk], sems.at[index])


def columns(s):
    return slice(None), pl.ds(pl.multiple_of(s * 3712, 128), 3712)


def rolled(value, turn):
    return pltpu.roll(value, turn, 1) if turn else value


def table_split_kernel(t_hbm, _, own_ref, send_ref, t_ref, sems):
    _, _, core = position()
    lane = lanes(64)
    for s in range(4):
        chunk_copy(t_hbm, t_ref, sems, s, columns(s)).start()

    def split(outs):
        def quarter(s, carry):
            chunk_copy(t_hbm, t_ref, sems, s, columns(s)).wait()
            base = pl.multiple_of(s * 3712, 128)
            for d in range(16):
                start, shift = 232 * d // 128, 232 * d % 128
                count = -(-(shift + 232) // 128)
                tiles = [
                    rolled(t_ref[:, pl.ds(base + 128 * (start + i), 128)], -shift % 128)
                    for i in range(count)
                ]
                for i in range(2):
                    v = tiles[i]
                    if shift and i + 1 < count:
                        v = jnp.where(lane < 128 - shift, v, tiles[i + 1])
                    if i == 1:
                        v = jnp.where(lane < 104, v, jnp.zeros_like(v))
                    outs[d % 2][s, d // 2, 64 * i : 64 * i + 64, :] = v
            return carry

        lax.fori_loop(0, 4, quarter, 0)

    pl.when(core == 0)(lambda: split((own_ref, send_ref)))
    pl.when(core == 1)(lambda: split((send_ref, own_ref)))


def split_kernel(q_hbm, o_hbm, own_ref, send_ref, tick_ref, q_ref, o_ref, q_sems, o_sems):
    _, x, core = position()
    lane = lanes(64)
    lane16 = lanes(16)

    def rows(s):
        return pl.ds(pl.multiple_of(s * 32, 32), 32), slice(None)

    tick_ref[...] = jnp.zeros_like(tick_ref)
    for s in range(4):
        chunk_copy(q_hbm, q_ref, q_sems, s, rows(s)).start()
        chunk_copy(o_hbm, o_ref, o_sems, s, columns(s)).start()

    def split(outs):
        def group(s, carry):
            chunk_copy(q_hbm, q_ref, q_sems, s, rows(s)).wait()
            chunk_copy(o_hbm, o_ref, o_sems, s, columns(s)).wait()
            half = s // 2
            for p in range(2):
                slot = (2 * (s % 2) + p) ^ x
                v = q_ref[pl.ds(pl.multiple_of(s * 32 + 16 * p, 16), 16), :]
                for c in range(2):
                    out_ref = outs[c]
                    part = v[8 * c : 8 * c + 8]
                    for t in range(16):
                        low = part[:, 128 * t : 128 * t + 128]
                        t2 = t + 16
                        high = part[:, 128 * t2 : 128 * t2 + 128] if t2 < QT else jnp.zeros_like(low)
                        out_ref[half, slot, 16 * t : 16 * t + 16, :] = jnp.concatenate(
                            [low, high], axis=0
                        )
                    b = 2 * p + c
                    shift = 32 * b
                    base = s * 3712 + 128 * (29 * b // 4)
                    tiles = [
                        rolled(
                            o_ref[:, pl.ds(pl.multiple_of(base + 128 * t, 128), 128)],
                            -shift % 128,
                        )
                        for t in range(8)
                    ]
                    for t in range(7):
                        w = jnp.where(lane < 128 - shift, tiles[t], tiles[t + 1]) if b else tiles[t]
                        first = QROWS + 64 * t
                        out_ref[half, slot, first : first + 64, :] = w
                    last = tiles[7]
                    rest = last[0:16]
                    for g in range(1, 4):
                        piece = pltpu.roll(last[16 * g : 16 * g + 16], 32 * g, 1)
                        rest = jnp.where(lane16 < 32 * g, rest, piece)
                    out_ref[half, slot, QROWS + 448 : QROWS + 464, :] = rest
            return carry

        lax.fori_loop(0, 4, group, 0)

    pl.when(core == 0)(lambda: split((own_ref, send_ref)))
    pl.when(core == 1)(lambda: split((send_ref, own_ref)))


def adamw(gradient, master, first, second, factor):
    clipped = gradient * factor
    first_new = beta_first * first + (1.0 - beta_first) * clipped
    second_new = beta_second * second + (1.0 - beta_second) * clipped * clipped
    first_hat = first_new / (1.0 - beta_first**STEP)
    second_hat = second_new / (1.0 - beta_second**STEP)
    master_new = master - learn_rate * (
        first_hat / (jnp.sqrt(second_hat) + tiny_value) + weight_decay * master
    )
    return master_new, first_new, second_new


def update_kernel(limit):
    def kernel(
        n_ref, g_ref,
        qw_ref, qm_ref, qv_ref, ow_ref, om_ref, ov_ref, tw_ref, tm_ref, tv_ref,
        pack_ref,
        qw2_ref, qm2_ref, qv2_ref, ow2_ref, om2_ref, ov2_ref, tw2_ref, tm2_ref, tv2_ref,
    ):
        grad_norm = jnp.sqrt(jnp.sum(n_ref[...], keepdims=True))
        factor = jnp.minimum(1.0, limit / (grad_norm + 1e-06))

        def step(g, rows, cols, refs, outs):
            new = adamw(g, *(r[rows, cols] for r in refs), factor)
            for ref, value in zip(outs, new):
                ref[rows, cols] = value
            return new[0]

        refs, outs = (qw_ref, qm_ref, qv_ref), (qw2_ref, qm2_ref, qv2_ref)
        every = slice(None)
        new = [
            step(
                g_ref[16 * (t % 16) + 8 * (t // 16) : 16 * (t % 16) + 8 * (t // 16) + 8, :],
                every, slice(128 * t, 128 * t + 128), refs, outs,
            )
            for t in range(QT)
        ]
        new.append(jnp.zeros_like(new[0]))
        for t in range(16):
            pack_ref[16 * t : 16 * t + 16, :] = jnp.concatenate(
                [new[t], new[t + 16]], axis=0
            ).astype(BF16)

        refs, outs = (ow_ref, om_ref, ov_ref), (ow2_ref, om2_ref, ov2_ref)
        for t in range(7):
            g = g_ref[QROWS + 64 * t : QROWS + 64 * t + 64, :]
            w = step(g, every, slice(128 * t, 128 * t + 128), refs, outs)
            pack_ref[QROWS + 64 * t : QROWS + 64 * t + 64, :] = w.astype(BF16)
        rest = g_ref[QROWS + 448 : QROWS + 464, :]
        lane = lanes(16)
        packed = jnp.zeros((16, 128), F32)
        for g in range(4):
            piece = rest if g == 0 else pltpu.roll(rest, 128 - 32 * g, 1)
            w = step(piece[:, 0:32], slice(16 * g, 16 * g + 16), slice(896, 928), refs, outs)
            w = jnp.concatenate([w, jnp.zeros((16, 96), F32)], axis=1)
            w = w if g == 0 else pltpu.roll(w, 32 * g, 1)
            packed = jnp.where((lane >= 32 * g) & (lane < 32 * g + 32), w, packed)
        pack_ref[QROWS + 448 : QROWS + 464, :] = packed.astype(BF16)

        refs, outs = (tw_ref, tm_ref, tv_ref), (tw2_ref, tm2_ref, tv2_ref)
        w = step(g_ref[PACK : PACK + 64, :], every, slice(0, 128), refs, outs)
        pack_ref[PACK : PACK + 64, :] = w.astype(BF16)
        w = step(g_ref[PACK + 64 : PACK + 128, 0:104], every, slice(128, 232), refs, outs)
        pack_ref[PACK + 64 : PACK + 128, :] = jnp.concatenate([w, jnp.zeros((64, 24), F32)], axis=1).astype(BF16)

    return kernel


def cover(t, width, count):
    found = []
    for b in range(count):
        begin = 128 * t - width * b
        for i in range(-(-width // 128)):
            lo = max(0, 128 * i - begin)
            hi = min(128, 128 * i - begin + 128, width - begin)
            if lo < hi:
                found.append((b, i, (-begin) % 128, lo, hi))
    return found


def join_kernel(own_ref, got_ref, _, q_hbm, o_hbm, q_ref, o_ref, q_sems, o_sems):
    zh, x, core = position()
    lane = lanes(64)

    def row_copy(j):
        chunk = pl.ds(pl.multiple_of(j * 16, 16), 16), slice(None)
        return chunk_copy(q_ref, q_hbm, q_sems, j, chunk)

    def join(refs):
        def rows(j, carry):
            index = (zh ^ (j // 4), x ^ (j % 4))
            for p in range(16):
                a, b = (ref[(*index, slice(16 * p, 16 * p + 16), slice(None))] for ref in refs)
                for t, part in ((p, slice(0, 8)), (p + 16, slice(8, 16))):
                    if t < QT:
                        q_ref[pl.ds(pl.multiple_of(j * 16, 16), 16), 128 * t : 128 * t + 128] = (
                            jnp.concatenate([a[part], b[part]], axis=0)
                        )
            row_copy(j).start()
            return carry

        lax.fori_loop(0, 8, rows, 0)

        def cols(g, carry):
            index = [
                (zh ^ (g // 2), x ^ (2 * (g % 2) + b // 2))
                for b in range(4)
            ]

            def tile(b, i, turn):
                if i < 7:
                    rows = slice(QROWS + 64 * i, QROWS + 64 * i + 64)
                    v = refs[b % 2][(*index[b], rows, slice(None))]
                    return pltpu.roll(v, turn, 1) if turn else v
                v = refs[b % 2][(*index[b], slice(QROWS + 448, QROWS + 464), slice(None))]
                parts = []
                for k in range(4):
                    move = (turn - 32 * k) % 128
                    parts.append(pltpu.roll(v, move, 1) if move else v)
                return jnp.concatenate(parts, axis=0)

            base = pl.multiple_of(g * 3712, 128)
            for t in range(29):
                value = None
                for b, i, turn, lo, hi in cover(t, 928, 4):
                    v = tile(b, i, turn)
                    value = v if value is None else jnp.where(lane >= lo, v, value)
                o_ref[:, pl.ds(base + 128 * t, 128)] = value
            chunk_copy(o_ref, o_hbm, o_sems, g, columns(g)).start()
            return carry

        lax.fori_loop(0, 4, cols, 0)

    pl.when(core == 0)(lambda: join((own_ref, got_ref)))
    pl.when(core == 1)(lambda: join((got_ref, own_ref)))
    for j in range(8):
        row_copy(j).wait()
    for g in range(4):
        chunk_copy(o_ref, o_hbm, o_sems, g, columns(g)).wait()


def table_join_kernel(own_ref, got_ref, t_hbm, tick_ref, t_ref, sems):
    tick_ref[...] = jnp.zeros_like(tick_ref)
    zh, x, core = position()
    section = lax.axis_index("section")
    lane = lanes(64)

    def join(refs):
        def quarter(s, carry):
            m = (section - s + 4) % 4
            base = pl.multiple_of(s * 3712, 128)
            for t in range(29):
                value = None
                for d, i, turn, lo, hi in cover(t, 232, 16):
                    index = (m, x ^ ((d // 2) % 4), zh ^ (d // 8))
                    rows = slice(64 * i, 64 * i + 64)
                    v = refs[d % 2][(*index, rows, slice(None))]
                    v = pltpu.roll(v, turn, 1) if turn else v
                    value = v if value is None else jnp.where(lane >= lo, v, value)
                t_ref[:, pl.ds(base + 128 * t, 128)] = value
            chunk_copy(t_ref, t_hbm, sems, s, columns(s)).start()
            return carry

        lax.fori_loop(0, 4, quarter, 0)

    pl.when(core == 0)(lambda: join((own_ref, got_ref)))
    pl.when(core == 1)(lambda: join((got_ref, own_ref)))
    for s in range(4):
        chunk_copy(t_ref, t_hbm, sems, s, columns(s)).wait()


def per_device(
    query_grads,
    query_master,
    query_first,
    query_second,
    output_grads,
    output_master,
    output_first,
    output_second,
    table_grads,
    table_master,
    table_first,
    table_second,
):
    section = lax.axis_index("section")
    member = lax.axis_index("dp")
    zh, x = member // 8, (member // 2) % 4
    query, output, table = query_grads[0, 0], output_grads[0, 0], table_grads[0, 0]

    def dp_send(value, perm):
        return lax.ppermute(value, "dp", perm)

    def pick(value, i):
        return lax.dynamic_index_in_dim(value, i, 0, False)

    own, send, tick = call(
        split_kernel, [out((2, 4, PACK, 128), BF16)] * 2 + [out((8, 128), F32)], query, output,
        hbm=(0, 1), micros=3, vmem=60,
        scratch=[
            pltpu.VMEM((128, 3968), BF16), pltpu.VMEM((64, 14848), BF16),
            pltpu.SemaphoreType.DMA((4,)), pltpu.SemaphoreType.DMA((4,)),
        ],
    )
    got = dp_send(send, CORE)
    t_own, t_send = call(
        table_split_kernel, [out((4, 8, TROWS, 128), BF16)] * 2, table, tick, hbm=(0,),
        scratch=[pltpu.VMEM((64, 14848), BF16), pltpu.SemaphoreType.DMA((4,))],
    )

    def slots(h, e):
        return own[h, e].astype(F32) + got[h, e].astype(F32)

    near, wrap = slots(0, slice(1, 3)).astype(F16), slots(1, slice(2, 4)).astype(F16)
    near, wrap, t_send = lax.optimization_barrier((near, wrap, t_send))
    t_got = dp_send(t_send, CORE)
    near = dp_send(near, x_perm(1))
    wrap = dp_send(wrap, x_perm(3))
    near_last = dp_send((slots(0, 3) + near[1].astype(F32)).astype(F16), x_perm(3)).astype(F32)
    wrap_last = dp_send((slots(1, 1) + wrap[0].astype(F32)).astype(F16), x_perm(1)).astype(F32)
    halves = (
        slots(0, 0) + near[0].astype(F32) + near_last,
        slots(1, 0) + wrap[1].astype(F32) + wrap_last,
    )

    first_section = section == 0
    at_ends = jnp.logical_or(first_section, section == 3)

    def quarter(i):
        return pick(t_own, i).astype(F32) + pick(t_got, i).astype(F32)

    def section_send(i, perm):
        return lax.ppermute(quarter(i).astype(F16), "section", perm)

    t_near = section_send(jnp.where(first_section, 1, 2), [(0, 1), (3, 2)])
    t_end = section_send(jnp.where(first_section, 3, 0), [(0, 3), (3, 0)])
    t_far = section_send(jnp.where(first_section, 2, 1), [(0, 2), (3, 1)])
    t_sum = jnp.where(at_ends, quarter(section), t_near.astype(F32)) + jnp.where(
        at_ends, t_end, t_far
    ).astype(F32)
    t_sum = t_sum.reshape(2, 4, TROWS, 128)

    def t_slot(k):
        return lax.dynamic_index_in_dim(t_sum, x ^ k, 1, False)

    t_parts = [t_slot(0)] + [dp_send(t_slot(k).astype(F16), x_perm(k)) for k in (1, 2, 3)]

    first_half = zh == 0

    def t_half(i):
        return sum(pick(v, i).astype(F32) for v in t_parts)

    leave = jnp.concatenate([jnp.where(first_half, halves[1], halves[0]), t_half(1 - zh)])
    keep = jnp.concatenate([jnp.where(first_half, halves[0], halves[1]), t_half(zh)])
    gradient = keep + dp_send(leave.astype(F16), ZHALF).astype(F32)

    squares = jnp.sum((gradient * gradient).reshape(-1, 8, 128), axis=0)
    squares = squares + dp_send(squares, CORE)
    squares = squares + sum(dp_send(squares, x_perm(k)) for k in (1, 2, 3))
    squares = squares + sum(lax.ppermute(squares, "section", ring_perm(k)) for k in (1, 2, 3))
    squares = squares + sum(lax.ppermute(squares, "tensor", line_perm(e)) for e in (1, 2, 3))
    squares = squares + dp_send(squares, ZHALF)

    params_count = 4 * (128 * 15872 + 256 * 14848) + 256 * 14848
    limit = 0.5 * math.sqrt(params_count)
    small = [out((8, 3968), F32)] * 3 + [out((64, 928), F32)] * 3 + [out((64, 232), F32)] * 3
    packed, *new = call(
        update_kernel(limit),
        (out((PACK + TROWS, 128), BF16), *small),
        squares, gradient,
        query_master[0], query_first[0], query_second[0],
        output_master[0], output_first[0], output_second[0],
        table_master, table_first, table_second,
    )

    def along_x(value):
        return jnp.stack([value] + [dp_send(value, x_perm(k)) for k in (1, 2, 3)])

    packed = jnp.stack([packed, dp_send(packed, ZHALF)])
    t_all = along_x(packed[:, PACK:])
    upper, lower = packed[:, :UPPER], packed[:, UPPER:PACK]
    upper_wrap = dp_send(upper, x_perm(3))
    lower_near = dp_send(lower, x_perm(1))
    _, upper_wrap, lower_near = lax.optimization_barrier((t_all, upper_wrap, lower_near))
    t_all = jnp.stack([t_all] + [lax.ppermute(t_all, "section", ring_perm(k)) for k in (1, 2, 3)])
    upper_rest = dp_send(jnp.stack([upper, upper_wrap]), x_perm(1))
    lower_rest = dp_send(jnp.stack([lower, lower_near]), x_perm(3))
    _, upper_rest, lower_rest = lax.optimization_barrier((t_all, upper_rest, lower_rest))
    w_all = jnp.concatenate(
        [
            jnp.stack([upper, upper_rest[0], upper_rest[1], upper_wrap], axis=1),
            jnp.stack([lower, lower_near, lower_rest[1], lower_rest[0]], axis=1),
        ],
        axis=2,
    )
    t_other = dp_send(t_all, CORE)
    t_other, w_all = lax.optimization_barrier((t_other, w_all))
    w_other = dp_send(w_all, CORE)
    table_full, tick = call(
        table_join_kernel, (out((64, 14848), BF16), out((8, 128), F32)), t_all, t_other,
        out_hbm=(0,), scratch=[pltpu.VMEM((64, 14848), BF16), pltpu.SemaphoreType.DMA((4,))],
    )
    query_full, output_full = call(
        join_kernel, (out((128, 3968), BF16), out((64, 14848), BF16)),
        w_all, w_other, tick, micros=3, out_hbm=(0, 1),
        scratch=[
            pltpu.VMEM((128, 3968), BF16), pltpu.VMEM((64, 14848), BF16),
            pltpu.SemaphoreType.DMA((8,)), pltpu.SemaphoreType.DMA((4,)),
        ],
    )
    return (
        query_full[None],
        *(a[None] for a in new[0:3]),
        output_full[None],
        *(a[None] for a in new[3:6]),
        table_full,
        *new[6:9],
    )


def solution(mesh):
    return jax.shard_map(
        per_device,
        mesh=mesh,
        in_specs=(
            P("section", "dp", None, "tensor"),
            P("section", "dp", "tensor"),
            P("section", "dp", "tensor"),
            P("section", "dp", "tensor"),
            P("section", "dp", "tensor", None),
            P("section", "tensor", "dp"),
            P("section", "tensor", "dp"),
            P("section", "tensor", "dp"),
            P("section", "dp", "tensor", None),
            P("tensor", ("section", "dp")),
            P("tensor", ("section", "dp")),
            P("tensor", ("section", "dp")),
        ),
        out_specs=(
            P("section", None, "tensor"),
            P("section", "dp", "tensor"),
            P("section", "dp", "tensor"),
            P("section", "dp", "tensor"),
            P("section", "tensor", None),
            P("section", "tensor", "dp"),
            P("section", "tensor", "dp"),
            P("section", "tensor", "dp"),
            P("tensor", None),
            P("tensor", ("section", "dp")),
            P("tensor", ("section", "dp")),
            P("tensor", ("section", "dp")),
        ),
        check_vma=False,
    )
```
